32 devices in a mesh: energy: 4 (over z), cols: 8 (over y, x, core).
Axes of the slice: x: 2, y: 2, z: 4, core: 2. Of those that a mesh axis runs over, the one named last changes fastest.
Arguments:
- left_inverse: bfloat16 [12, 2, 1536, 1536], P('energy', None, 'cols'), parts along dimension 0, as said below
- regions: int32 [3, 1536], replicated, may hold values from 0 to 2
- region_mass: float32 [3], replicated, may hold values from 1 to 2.5
- region_alpha: float32 [3], replicated, may hold values from 0.1 to 0.5
- energy_grid: float32 [16], replicated, may hold values from 0.2 to 1
- energy_index: int32 [4], P('energy'), parts along dimension 0, may hold values from 0 to 15
Outputs:
- green: float32 [8, 2, 1536, 1536], P('energy', None, 'cols'), parts along dimension 0
The draws below stay inside these ranges and needn't reach their ends.
There are 4 independent parts, one for each index of `energy`. The reference program is written for one: setup_inputs(seed, part) draws one part's arguments, and reference() takes and returns one part's arrays. A program takes and returns all parts, laid end to end along the dimension named above; an argument that names none is the same for every part. Nothing has to cross between parts.
Inputs may be any that keep to these rules, and one draw needn't show every extreme that they name: Every block of left_inverse is complex symmetric: both planes equal their transposes.
All inputs are finite; a program needn't handle non-finite values.
Results may differ from the reference program's by a relative error of at most 0.0024.
Values may be sent and summed in bfloat16 or wider, within the bound.
No kernel may reach another device: no remote copies, remote signals or barrier semaphores. Data moves between devices by JAX's collectives and lax.ppermute only.
A program may use at most 128 MiB of HBM per device.

```python
import math
import jax
import jax.numpy as jnp

P_SIZE = 1536
SLICES = 3
REGIONS = 3
NE = 16


def draw_left_inverse(key, part):
    keys = jax.random.split(jax.random.fold_in(key, 7), 3)
    shape = (SLICES, 2, P_SIZE, P_SIZE)
    noise = jax.random.normal(keys[0], shape, jnp.float32)
    noise = noise * (0.6 / P_SIZE ** 0.5)
    symmetric = (noise + jnp.swapaxes(noise, 2, 3)) * 0.70710678
    real_diag = jax.random.uniform(keys[1], (SLICES, 1, P_SIZE), jnp.float32, 0.5, 1.2)
    imag_diag = jax.random.uniform(keys[2], (SLICES, 1, P_SIZE), jnp.float32, -0.8, -0.2)
    diagonal = jnp.concatenate([real_diag, imag_diag], axis=1)
    identity = jnp.eye(P_SIZE, dtype=jnp.float32)
    block = symmetric * (1.0 - identity) + identity * diagonal[:, :, :, None]
    return block.astype(jnp.bfloat16)


def touch_ends(values, own_key, smallest, top_value):
    longest = values.shape.index(max(values.shape))
    spots = []
    for shift in (0, 1):
        where = [jax.random.randint(jax.random.fold_in(own_key, axis), (), 0, length) for axis, length in enumerate(values.shape)]
        where[longest] = (where[longest] + shift) % values.shape[longest]
        spots.append(tuple(where))
    return values.at[spots[0]].set(smallest).at[spots[1]].set(top_value)


def setup_inputs(seed: int = 0, part: int = 0) -> dict:
    streams_of = jax.random.split(jax.random.key(seed), 7)
    part_splits = jax.random.split(jax.random.fold_in(streams_of[6], part), 7)
    left_inverse = draw_left_inverse(jax.random.fold_in(jax.random.fold_in(streams_of[6], part), 71), part)
    regions = touch_ends(jax.random.randint(streams_of[1], (SLICES, P_SIZE), 0, REGIONS), jax.random.fold_in(streams_of[1], 1), 0, REGIONS - 1).astype(jnp.int32)
    region_mass = jnp.clip(jnp.exp(jax.random.uniform(streams_of[2], (REGIONS,), jnp.float32, math.log(1.0), math.log(2.5))), 1.0, 2.5)
    region_alpha = jnp.clip(jnp.exp(jax.random.uniform(streams_of[3], (REGIONS,), jnp.float32, math.log(0.1), math.log(0.5))), 0.1, 0.5)
    energy_grid = jnp.clip(jax.random.uniform(streams_of[4], (NE,), jnp.float32, 0.2, 1.0), 0.2, 1.0)
    energy_index = jax.random.randint(part_splits[5], (1,), 0, NE).astype(jnp.int32)
    return {"left_inverse": left_inverse, "regions": regions, "region_mass": region_mass, "region_alpha": region_alpha, "energy_grid": energy_grid, "energy_index": energy_index}


def complex_product(left, right):
    real = jnp.dot(left[0], right[0], preferred_element_type=jnp.float32) - jnp.dot(left[1], right[1], preferred_element_type=jnp.float32)
    imag = jnp.dot(left[0], right[1], preferred_element_type=jnp.float32) + jnp.dot(left[1], right[0], preferred_element_type=jnp.float32)
    return jnp.stack([real, imag])


def couplings(regions, region_mass, region_alpha, energy_grid, energy_index):
    level = jnp.sum(jnp.where(jnp.arange(energy_grid.shape[0]) == energy_index[0], energy_grid, 0.0))
    onehot = (regions[:, :, None] == jnp.arange(region_mass.shape[0])[None, None, :]).astype(jnp.float32)
    per_region = region_mass * (1.0 + region_alpha * level)
    mass = jnp.sum(onehot * per_region[None, None, :], axis=2)
    return 2.0 / (mass[:-1] + mass[1:])


def reference(left_inverse, regions, region_mass, region_alpha, energy_grid, energy_index):
    hop = couplings(regions, region_mass, region_alpha, energy_grid, energy_index)
    count = left_inverse.shape[0]
    next_green = left_inverse[count - 1]
    blocks = []
    for index in range(count - 2, -1, -1):
        panel = left_inverse[index]
        factor = hop[index][None, :, None]
        scaled = (factor * panel.astype(jnp.float32)).astype(jnp.bfloat16)
        image = (factor * complex_product(next_green, scaled)).astype(jnp.bfloat16)
        current = panel.astype(jnp.float32) + complex_product(panel, image)
        blocks.append(current)
        next_green = current.astype(jnp.bfloat16)
    return jnp.stack(blocks[::-1])
```

```python
import functools

import jax
import jax.numpy as jnp
from jax import lax
from jax.experimental import pallas as pl
from jax.experimental.pallas import tpu as pltpu
from jax.sharding import PartitionSpec as P

F32 = jnp.float32
BF16 = jnp.bfloat16
F8 = jnp.float8_e5m2
F8_MAX = 57344.0
LOW = 512.0
DIAG = 16
ORDER = (1, 2, 0)
PAD = 16
VMEM = pl.BlockSpec(memory_space=pltpu.VMEM)
SMEM = pl.BlockSpec(memory_space=pltpu.SMEM)
ANY = pl.BlockSpec(memory_space=pl.ANY)
HBM = pl.BlockSpec(memory_space=pltpu.HBM)


def params(mib=56):
    return pltpu.CompilerParams(vmem_limit_bytes=mib * 2**20)


def cost(flops, moved):
    return pl.CostEstimate(flops=flops, bytes_accessed=moved, transcendentals=0)


def couplings(regions, region_mass, region_alpha, energy_grid, energy_index):
    level = jnp.sum(
        jnp.where(jnp.arange(energy_grid.shape[0]) == energy_index[0], energy_grid, 0.0)
    )
    onehot = (regions[:, :, None] == jnp.arange(region_mass.shape[0])[None, None, :]).astype(F32)
    per_region = region_mass * (1.0 + region_alpha * level)
    mass = jnp.sum(onehot * per_region[None, None, :], axis=2)
    return 2.0 / (mass[:-1] + mass[1:])


def product(left, right):
    real = jnp.dot(left[0], right[0], preferred_element_type=F32) - jnp.dot(
        left[1], right[1], preferred_element_type=F32
    )
    imag = jnp.dot(left[0], right[1], preferred_element_type=F32) + jnp.dot(
        left[1], right[0], preferred_element_type=F32
    )
    return jnp.stack([real, imag])


def general(left_inverse, regions, region_mass, region_alpha, energy_grid, energy_index):
    hop = couplings(regions, region_mass, region_alpha, energy_grid, energy_index)
    count = left_inverse.shape[0]
    whole = [None] * count
    for index in list(range(count - 2, -1, -1)) + [count - 1]:
        whole[index] = lax.all_gather(left_inverse[index], "cols", axis=1, tiled=True)
    blocks = []
    for index in range(count - 2, -1, -1):
        rows = left_inverse[index].astype(F32)

        def times_green(left, level):
            if level == count - 1:
                return product(left, whole[level])
            first = product(left, whole[level])
            inner = times_green((first * hop[level]).astype(BF16), level + 1)
            return first + product((inner * hop[level]).astype(BF16), whole[level])

        inner = times_green((rows * hop[index]).astype(BF16), index + 1)
        blocks.append(rows + product((inner * hop[index]).astype(BF16), whole[index]))
    return jnp.stack(blocks[::-1])


TILE = 512
LIMITS = (16, 16, 22, 24, 20)


class Sizes:
    def __init__(self, rows, size):
        self.rows = rows
        self.chip = 2 * rows
        self.size = size
        self.head = rows + DIAG
        self.slab = rows * 4 + DIAG


def own_part(idx_ref):
    index = idx_ref[0]
    return lax.div(index, 2), lax.rem(index, 2)


def columns(chip, other, s):
    return pl.ds(pl.multiple_of(jnp.bitwise_xor(chip, other) * s.chip, 128), s.chip)


class Copies:
    def __init__(self, sems):
        self.sems = sems
        self.made = []

    def start(self, source, target):
        copy = pltpu.make_async_copy(source, target, self.sems.at[len(self.made)])
        copy.start()
        self.made.append([copy, False])
        return len(self.made) - 1

    def wait(self, which=None):
        for i in range(len(self.made)) if which is None else which:
            copy, done = self.made[i]
            if not done:
                copy.wait()
                self.made[i][1] = True


def pack_kernel(s, index, heads, idx_ref, a_ref, *refs):
    n = 3 if heads else 2
    outs, buffers, (planes, sems) = refs[:n], refs[n : 2 * n], refs[2 * n :]
    xs, ys = buffers[:2]
    chip, core = own_part(idx_ref)
    r = s.rows
    copies = Copies(sems)
    blocks = heads or (index,)
    loads = [
        copies.start(a_ref.at[block, :, :, columns(chip, 0, s)], planes.at[i])
        for i, block in enumerate(blocks)
    ]
    for plane in (0, 1):
        here = pl.ds(s.head + plane * r, r)
        copies.start(a_ref.at[index, plane, :, columns(chip, 2, s)], xs.at[here, :])
        copies.start(a_ref.at[index, plane, :, columns(chip, 1, s)], ys.at[here, :])
    here = pl.ds(s.head + 2 * r, r)
    copies.start(a_ref.at[index, 0, :, columns(chip, 3, s)], xs.at[here, :])
    copies.start(a_ref.at[index, 1, :, columns(chip, 3, s)], ys.at[here, :])
    row = lax.broadcasted_iota(jnp.int32, (r, s.chip), 0) + core * r
    col = lax.broadcasted_iota(jnp.int32, (r, s.chip), 1)
    for i, block in enumerate(blocks):
        copies.wait([loads[i]])
        real = planes[i, 0].astype(F32)
        imag = planes[i, 1].astype(F32)
        head = jnp.where(col >= row, real, imag).astype(BF16)
        diag = jnp.sum(jnp.where(col == row, imag, 0.0), axis=0, keepdims=True)
        diag = jnp.broadcast_to(diag, (DIAG, s.chip)).astype(BF16)
        places = [(xs, 0), (ys, 0)] if block == index else []
        if heads:
            places.append((buffers[2], i * s.head))
        for buffer, start in places:
            buffer[start : start + r, :] = head
            buffer[start + r : start + s.head, :] = diag
    for buffer in (xs, ys):
        if buffer.shape[0] > s.slab:
            buffer[s.slab :, :] = jnp.zeros((buffer.shape[0] - s.slab, s.chip), BF16)
    copies.wait()
    for buffer, out in zip(buffers, outs):
        copies.start(buffer, out)
    copies.wait()


def pack(s, idx, a, index, heads):
    rows = s.slab + PAD * ORDER.index(index)
    shapes = [jax.ShapeDtypeStruct((k, s.chip), BF16) for k in (rows, rows, len(heads) * s.head)]
    if not heads:
        shapes.pop()
    return list(
        pl.pallas_call(
            functools.partial(pack_kernel, s, index, heads),
            in_specs=[SMEM, HBM],
            out_specs=[ANY] * len(shapes),
            out_shape=shapes,
            scratch_shapes=[pltpu.VMEM(x.shape, BF16) for x in shapes]
            + [
                pltpu.VMEM((max(1, len(heads)), 2, s.rows, s.chip), BF16),
                pltpu.SemaphoreType.DMA((12,)),
            ],
            compiler_params=params(LIMITS[0]),
            cost_estimate=cost(0, 0),
            name="pack",
        )(idx, a)
    )


def gate_kernel(*refs):
    pass


def gate(buffers, tokens):
    n = len(buffers)
    return list(pl.pallas_call(
        gate_kernel,
        in_specs=[ANY] * (n + len(tokens)),
        out_specs=[ANY] * n,
        out_shape=[jax.ShapeDtypeStruct(b.shape, b.dtype) for b in buffers],
        input_output_aliases={i: i for i in range(n)},
        compiler_params=params(1),
        cost_estimate=cost(0, 0),
        name="gate",
    )(*buffers, *tokens))


def put_split(hi_ref, lo_ref, rows, cols, value):
    hi = value.astype(BF16)
    hi_ref[rows, cols] = hi
    if lo_ref is None:
        return
    rest = (value - hi.astype(F32)) * LOW
    lo_ref[rows, cols] = jnp.clip(rest, -F8_MAX, F8_MAX).astype(F8)


def prep_kernel(
    s, idx_ref, index_ref, grid_ref, mass_ref, alpha_ref, regions_ref, a_ref, _, hop_out, down_out, s0_hi, s0_lo, s1_ref
):
    chip, _ = own_part(idx_ref)
    r = s.rows
    level = grid_ref[index_ref[0]]
    for other in range(4):
        cols = columns(chip, other, s)
        regions = regions_ref[:, cols]
        mass = jnp.zeros(regions.shape, F32)
        for region in range(mass_ref.shape[0]):
            value = mass_ref[region] * (1.0 + alpha_ref[region] * level)
            mass = jnp.where(regions == region, value, mass)
        hop = 2.0 / (mass[:-1] + mass[1:])
        here = slice(other * s.chip, (other + 1) * s.chip)
        hop_out[:, here] = hop
        for index in (0, 1):
            down_out[index, here, :] = jnp.broadcast_to(hop[index : index + 1, :], (128, s.chip)).T
            for plane in (0, 1):
                part = a_ref[index, plane, :, cols].astype(F32) * hop[index : index + 1, :]
                rows = slice(plane * r, (plane + 1) * r)
                hi, lo = ((s0_hi, s0_lo), (s1_ref, None))[index]
                put_split(hi, lo, rows, here, part)


def full(x):
    return pl.BlockSpec(x.shape, lambda i: (0,) * x.ndim)


def prep(s, idx, a, regions, region_mass, region_alpha, energy_grid, energy_index, token):
    shapes = [
        jax.ShapeDtypeStruct((regions.shape[0] - 1, regions.shape[1]), F32),
        jax.ShapeDtypeStruct((regions.shape[0] - 1, regions.shape[1], 128), F32),
    ] + split_shapes(s) + split_shapes(s)[:1]
    return pl.pallas_call(
        functools.partial(prep_kernel, s),
        grid=(1,),
        in_specs=[SMEM] * 5
        + [full(regions), pl.BlockSpec((2,) + a.shape[1:], lambda i: (0, 0, 0, 0)), ANY],
        out_specs=[full(x) for x in shapes],
        out_shape=shapes,
        compiler_params=params(16),
        cost_estimate=cost(0, 0),
        name="prep",
    )(idx, energy_index, energy_grid, region_mass, region_alpha, regions, a, token)


def split_shapes(s):
    return [jax.ShapeDtypeStruct((s.chip, s.size), kind) for kind in (BF16, F8)]


PIECES = 40


def start_pieces(s, chip, core, index, rows_refs, sides, z_at, whole, diags, copies):
    r, m = s.rows, s.chip

    def cols(other):
        return pl.ds(other * m, m)

    for side, (offset, ref, (xs, ys, z)) in enumerate(
        zip((core * r, (1 - core) * r), rows_refs, sides)
    ):

        def rows(base):
            return pl.ds(pl.multiple_of(base + offset, 16), r)

        for other in range(4):
            copies.start(
                ref.at[index, :, :, columns(chip, other, s)], whole.at[:, rows(0), cols(other)]
            )
        for which, got, at in ((1, xs, 0), (2, ys, 0), (3, z, z_at)):
            copies.start(got.at[pl.ds(at, r), :], whole.at[0, rows(which * m), cols(which)])
            copies.start(got.at[pl.ds(at + r, DIAG), :], diags.at[which - 1, side])
            if which == 3:
                continue
            for plane in (0, 1):
                copies.start(
                    got.at[pl.ds(s.head + plane * r, r), :],
                    whole.at[plane, rows(which * m), cols(3)],
                )
            copies.start(
                got.at[pl.ds(s.head + 2 * r, r), :],
                whole.at[which - 1, rows(which * m), cols(3 - which)],
            )


def complete(s, whole, diags):
    m = s.chip
    row = lax.broadcasted_iota(jnp.int32, (m, m), 0)
    col = lax.broadcasted_iota(jnp.int32, (m, m), 1)
    for which in (1, 2, 3):
        here = slice(which * m, (which + 1) * m)
        packed = whole[0, here, here].astype(F32)
        flipped = packed.T
        diag = diags[which - 1, 0].astype(F32) + diags[which - 1, 1].astype(F32)
        diag = jnp.broadcast_to(diag[0:1, :], (m, m))
        real = jnp.where(col >= row, packed, flipped)
        imag = jnp.where(col < row, packed, jnp.where(col > row, flipped, diag))
        whole[0, here, here] = real.astype(BF16)
        whole[1, here, here] = imag.astype(BF16)
    for plane in (0, 1):
        for a, b in ((0, 1), (0, 2), (0, 3), (1, 3), (2, 3), (1, 2) if plane == 0 else (2, 1)):
            block = whole[plane, a * m : (a + 1) * m, b * m : (b + 1) * m]
            whole[plane, b * m : (b + 1) * m, a * m : (a + 1) * m] = block.T


def multiply(lefts, right, s):
    r = s.rows
    if any(lo is not None for _, lo in lefts):
        small = [jnp.clip(plane, -F8_MAX, F8_MAX).astype(F8) for plane in right]
    out = []
    for hi, lo in lefts:
        by = [jnp.dot(hi[...], plane, preferred_element_type=F32) for plane in right]
        if lo is not None:
            by = [
                part + jnp.dot(lo[...], low, preferred_element_type=F32) * (1.0 / LOW)
                for part, low in zip(by, small)
            ]
        out.append((by[0][:r] - by[1][r:], by[1][:r] + by[0][r:]))
    return out


def planes(whole, cols):
    return [whole[plane, :, cols] for plane in (0, 1)]


def segments(start, width, s):
    at, out = start, []
    while at < start + width:
        other = at // s.chip
        stop = min(start + width, (other + 1) * s.chip)
        out.append((at, stop - at, other, at - other * s.chip))
        at = stop
    return out


def first_kernel(s, idx_ref, hop_ref, down_ref, hi, lo, *refs):
    own, own_c, x1, x1_c, y1, y1_c, z, z_c = refs[:8]
    scaled, x, w_hi, w_lo, whole, diags, sems = refs[8:]
    chip, core = own_part(idx_ref)
    r, n = s.rows, s.size
    copies = Copies(sems)
    sides = ((x1, y1, z), (x1_c, y1_c, z_c))
    start_pieces(s, chip, core, 1, (own, own_c), sides, 0, whole, diags, copies)
    copies.wait()
    complete(s, whole, diags)
    for t in range(0, n, TILE):
        cols = slice(t, t + TILE)
        right = planes(whole, cols)
        (parts,) = multiply([(hi, lo)], right, s)
        for plane, part in enumerate(parts):
            here = slice(plane * r, (plane + 1) * r)
            x[here, cols] = part
            put_split(w_hi, w_lo, here, cols, part * hop_ref[1:2, cols])
            scaled[plane, :, cols] = scale_rows(right[plane], down_ref, 1)


def scale_rows(plane, down_ref, index):
    return (plane.astype(F32) * down_ref[index, :, 0:1]).astype(BF16)


def second_kernel(s, idx_ref, s1_ref, w_hi, w_lo, *refs):
    own, own_c, x2, x2_c, y2, y2_c, z, z_c = refs[:8]
    u_ref, y_hi, y_lo, whole, diags, sems = refs[8:]
    chip, core = own_part(idx_ref)
    r, n = s.rows, s.size
    copies = Copies(sems)
    sides = ((x2, y2, z), (x2_c, y2_c, z_c))
    start_pieces(s, chip, core, 2, (own, own_c), sides, s.head, whole, diags, copies)
    copies.wait()
    complete(s, whole, diags)
    for t in range(0, n, TILE):
        cols = slice(t, t + TILE)
        u, y = multiply([(s1_ref, None), (w_hi, w_lo)], planes(whole, cols), s)
        for plane in (0, 1):
            here = slice(plane * r, (plane + 1) * r)
            put_split(u_ref, None, here, cols, u[plane])
            put_split(y_hi, y_lo, here, cols, y[plane])


def third_kernel(s, hi, lo, scaled, x, v_hi, v_lo):
    r, n = s.rows, s.size
    for t in range(0, n, TILE):
        cols = slice(t, t + TILE)
        (parts,) = multiply([(hi, lo)], planes(scaled, cols), s)
        for plane in (0, 1):
            here = slice(plane * r, (plane + 1) * r)
            put_split(v_hi, v_lo, here, cols, x[here, cols] + parts[plane])


def start_own(s, chip, a_ref, index, own, copies):
    return [
        copies.start(
            a_ref.at[index, :, :, columns(chip, other, s)],
            own.at[:, :, pl.ds(other * s.chip, s.chip)],
        )
        for other in range(4)
    ]


def green_kernel(s, idx_ref, left, scaled, a_ref, g1, own, sems):
    chip, core = own_part(idx_ref)
    copies = Copies(sems)
    mine = start_own(s, chip, a_ref, 1, own, copies)
    for t in range(0, s.size, TILE):
        (parts,) = multiply([(left, None)], planes(scaled, slice(t, t + TILE)), s)
        copies.wait(mine)
        add_own(s, own, parts, t, TILE, g1)


def add_own(s, own, parts, start, width, g_ref):
    cols = slice(start, start + width)
    for plane in (0, 1):
        g_ref[plane, :, cols] = own[plane, :, cols].astype(F32) + parts[plane]


def send_out(s, chip, start, width, g_ref, out_ref, index, copies):
    for at, size, other, offset in segments(start, width, s):
        base = jnp.bitwise_xor(chip, other) * s.chip + offset
        where = pl.ds(pl.multiple_of(base, 128), size)
        copies.start(g_ref.at[:, :, pl.ds(at, size)], out_ref.at[index, :, :, where])


def last_kernel(s, idx_ref, down_ref, hi, lo, g1, *refs):
    rows, rows_c, x0, x0_c, y0, y0_c, z, z_c = refs[:8]
    out_ref, whole, diags, own, g0, sems = refs[8:]
    chip, core = own_part(idx_ref)
    copies = Copies(sems)
    sides = ((x0, y0, z), (x0_c, y0_c, z_c))
    start_pieces(s, chip, core, 0, (rows, rows_c), sides, 0, whole, diags, copies)
    start_own(s, chip, rows, 0, own, copies)
    copies.wait()
    send_out(s, chip, 0, s.size, g1, out_ref, 1, copies)
    complete(s, whole, diags)
    width = TILE // 2
    for t in range(0, s.size, width):
        cols = slice(t, t + width)
        right = [scale_rows(plane, down_ref, 0) for plane in planes(whole, cols)]
        (parts,) = multiply([(hi, lo)], right, s)
        add_own(s, own, parts, t, width, g0)
        send_out(s, chip, t, width, g0, out_ref, 0, copies)
    copies.wait()


def swap(x, mask, n=8):
    return lax.ppermute(x, "cols", [(i, i ^ mask) for i in range(n)])


def special(left_inverse, regions, region_mass, region_alpha, energy_grid, energy_index):
    a = left_inverse
    s = Sizes(a.shape[2], a.shape[3])
    idx = lax.axis_index("cols").astype(jnp.int32)[None]
    n, m, r = s.size, s.chip, s.rows

    a_cross = swap(a, 1)
    x1, y1, z = pack(s, idx, a, 1, (1, 2))
    x1, y1, z = swap(x1, 2), swap(y1, 4), swap(z, 6)
    x2, y2 = pack(s, idx, a, 2, ())
    x0, y0, z0 = pack(s, idx, a, 0, (0,))
    hop, down, s0_hi, s0_lo, s1 = prep(
        s, idx, a, regions, region_mass, region_alpha, energy_grid, energy_index, a_cross
    )
    x1, y1, z = gate([x1, y1, z], (hop, x0, x2))
    x2, y2 = swap(x2, 2), swap(y2, 4)
    z_cross = swap(z, 1)

    split = split_shapes(s)
    block = jax.ShapeDtypeStruct((2, n, n), BF16)
    whole = pltpu.VMEM(block.shape, BF16)
    diags = pltpu.VMEM((3, 2, DIAG, m), BF16)
    own = pltpu.VMEM((2, r, n), BF16)
    sems = pltpu.SemaphoreType.DMA((PIECES + 20,))

    def call(kernel, name, ins, pieces, out_specs, out_shape, scratch, limit):
        return pl.pallas_call(
            functools.partial(kernel, s),
            in_specs=[SMEM if x is idx else HBM if x is a else VMEM for x in ins]
            + [HBM if x is a or x is a_cross else ANY for x in pieces],
            out_specs=out_specs,
            out_shape=out_shape,
            scratch_shapes=scratch,
            compiler_params=params(limit),
            cost_estimate=cost(0, 0),
            name=name,
        )(*ins, *pieces)

    scaled, x, w_hi, w_lo = call(
        first_kernel,
        "first",
        [idx, hop, down, s0_hi, s0_lo],
        [a, a_cross, x1, swap(x1, 1), y1, swap(y1, 1), z, z_cross],
        [VMEM] * 4,
        [block, jax.ShapeDtypeStruct((m, n), F32)] + split,
        [whole, diags, sems],
        LIMITS[1],
    )
    x0, y0, z0 = gate([x0, y0, z0], (z_cross,))
    x0, y0, z0 = swap(x0, 2), swap(y0, 4), swap(z0, 6)
    x2, y2 = gate([x2, y2], (w_hi,))
    u, y_hi, y_lo = call(
        second_kernel,
        "second",
        [idx, s1, w_hi, w_lo],
        [a, a_cross, x2, swap(x2, 1), y2, swap(y2, 1), z, z_cross],
        [VMEM] * 3,
        split[:1] + split,
        [whole, diags, sems],
        LIMITS[2],
    )
    v_hi, v_lo = call(
        third_kernel, "third", [y_hi, y_lo, scaled, x], [], [VMEM] * 2, split, [], LIMITS[3]
    )
    x0, y0, z0 = gate([x0, y0, z0], (v_hi,))
    green = jax.ShapeDtypeStruct((2, r, n), F32)
    g1 = call(
        green_kernel, "green_1", [idx, u, scaled, a], [], VMEM, green, [own, sems], LIMITS[3]
    )
    return call(
        last_kernel,
        "green_0",
        [idx, down, v_hi, v_lo, g1],
        [a, a_cross, x0, swap(x0, 1), y0, swap(y0, 1), z0, swap(z0, 1)],
        HBM,
        jax.ShapeDtypeStruct((2, 2, r, n), F32),
        [whole, diags, own, pltpu.VMEM((2, r, n), F32), sems],
        LIMITS[4],
    )


def solution(mesh):
    def on_device(left_inverse, *rest):
        rows = left_inverse.shape[2]
        if mesh.shape["cols"] == 8 and left_inverse.shape[0] == 3 and rows % 64 == 0:
            return special(left_inverse, *rest)
        return general(left_inverse, *rest)

    in_specs = (P("energy", None, "cols", None), P(), P(), P(), P(), P("energy"))
    out_specs = P("energy", None, "cols", None)
    return jax.shard_map(
        on_device, mesh=mesh, in_specs=in_specs, out_specs=out_specs, check_vma=False
    )
```

```python
import functools

import jax
import jax.numpy as jnp
from jax import lax
from jax.experimental import pallas as pl
from jax.experimental.pallas import tpu as pltpu
from jax.sharding import PartitionSpec as P

F32 = jnp.float32
BF16 = jnp.bfloat16
F8 = jnp.float8_e5m2
F8_MAX = 57344.0
LOW = 512.0
DIAG = 16
ORDER = (1, 2, 0)
PAD = 16
VMEM = pl.BlockSpec(memory_space=pltpu.VMEM)
SMEM = pl.BlockSpec(memory_space=pltpu.SMEM)
ANY = pl.BlockSpec(memory_space=pl.ANY)
HBM = pl.BlockSpec(memory_space=pltpu.HBM)


def params(mib=56):
    return pltpu.CompilerParams(vmem_limit_bytes=mib * 2**20)


def cost(flops, moved):
    return pl.CostEstimate(flops=flops, bytes_accessed=moved, transcendentals=0)


def couplings(regions, region_mass, region_alpha, energy_grid, energy_index):
    level = jnp.sum(
        jnp.where(jnp.arange(energy_grid.shape[0]) == energy_index[0], energy_grid, 0.0)
    )
    onehot = (regions[:, :, None] == jnp.arange(region_mass.shape[0])[None, None, :]).astype(F32)
    per_region = region_mass * (1.0 + region_alpha * level)
    mass = jnp.sum(onehot * per_region[None, None, :], axis=2)
    return 2.0 / (mass[:-1] + mass[1:])


def product(left, right):
    real = jnp.dot(left[0], right[0], preferred_element_type=F32) - jnp.dot(
        left[1], right[1], preferred_element_type=F32
    )
    imag = jnp.dot(left[0], right[1], preferred_element_type=F32) + jnp.dot(
        left[1], right[0], preferred_element_type=F32
    )
    return jnp.stack([real, imag])


def general(left_inverse, regions, region_mass, region_alpha, energy_grid, energy_index):
    hop = couplings(regions, region_mass, region_alpha, energy_grid, energy_index)
    count = left_inverse.shape[0]
    whole = [None] * count
    for index in list(range(count - 2, -1, -1)) + [count - 1]:
        whole[index] = lax.all_gather(left_inverse[index], "cols", axis=1, tiled=True)
    blocks = []
    for index in range(count - 2, -1, -1):
        rows = left_inverse[index].astype(F32)

        def times_green(left, level):
            if level == count - 1:
                return product(left, whole[level])
            first = product(left, whole[level])
            inner = times_green((first * hop[level]).astype(BF16), level + 1)
            return first + product((inner * hop[level]).astype(BF16), whole[level])

        inner = times_green((rows * hop[index]).astype(BF16), index + 1)
        blocks.append(rows + product((inner * hop[index]).astype(BF16), whole[index]))
    return jnp.stack(blocks[::-1])


TILE = 256
WIDE = 512
LIMITS = (16, 16, 22, 24, 20)


class Sizes:
    def __init__(self, rows, size):
        self.rows = rows
        self.chip = 2 * rows
        self.size = size
        self.head = rows + DIAG
        self.slab = rows * 4 + DIAG


def own_part(idx_ref):
    index = idx_ref[0]
    return lax.div(index, 2), lax.rem(index, 2)


def columns(chip, other, s):
    return pl.ds(pl.multiple_of(jnp.bitwise_xor(chip, other) * s.chip, 128), s.chip)


class Copies:
    def __init__(self, sems):
        self.sems = sems
        self.made = []

    def start(self, source, target):
        copy = pltpu.make_async_copy(source, target, self.sems.at[len(self.made)])
        copy.start()
        self.made.append([copy, False])
        return len(self.made) - 1

    def wait(self, which=None):
        for i in range(len(self.made)) if which is None else which:
            copy, done = self.made[i]
            if not done:
                copy.wait()
                self.made[i][1] = True


def pack_kernel(s, index, heads, idx_ref, a_ref, *refs):
    n = 3 if heads else 2
    outs, buffers, (planes, sems) = refs[:n], refs[n : 2 * n], refs[2 * n :]
    xs, ys = buffers[:2]
    chip, core = own_part(idx_ref)
    r = s.rows
    copies = Copies(sems)
    blocks = heads or (index,)
    loads = [
        copies.start(a_ref.at[block, :, :, columns(chip, 0, s)], planes.at[i])
        for i, block in enumerate(blocks)
    ]
    for plane in (0, 1):
        here = pl.ds(s.head + plane * r, r)
        copies.start(a_ref.at[index, plane, :, columns(chip, 2, s)], xs.at[here, :])
        copies.start(a_ref.at[index, plane, :, columns(chip, 1, s)], ys.at[here, :])
    here = pl.ds(s.head + 2 * r, r)
    copies.start(a_ref.at[index, 0, :, columns(chip, 3, s)], xs.at[here, :])
    copies.start(a_ref.at[index, 1, :, columns(chip, 3, s)], ys.at[here, :])
    row = lax.broadcasted_iota(jnp.int32, (r, s.chip), 0) + core * r
    col = lax.broadcasted_iota(jnp.int32, (r, s.chip), 1)
    for i, block in enumerate(blocks):
        copies.wait([loads[i]])
        real = planes[i, 0].astype(F32)
        imag = planes[i, 1].astype(F32)
        head = jnp.where(col >= row, real, imag).astype(BF16)
        diag = jnp.sum(jnp.where(col == row, imag, 0.0), axis=0, keepdims=True)
        diag = jnp.broadcast_to(diag, (DIAG, s.chip)).astype(BF16)
        places = [(xs, 0), (ys, 0)] if block == index else []
        if heads:
            places.append((buffers[2], i * s.head))
        for buffer, start in places:
            buffer[start : start + r, :] = head
            buffer[start + r : start + s.head, :] = diag
    for buffer in (xs, ys):
        if buffer.shape[0] > s.slab:
            buffer[s.slab :, :] = jnp.zeros((buffer.shape[0] - s.slab, s.chip), BF16)
    copies.wait()
    for buffer, out in zip(buffers, outs):
        copies.start(buffer, out)
    copies.wait()


def pack(s, idx, a, index, heads):
    rows = s.slab + PAD * ORDER.index(index)
    shapes = [jax.ShapeDtypeStruct((k, s.chip), BF16) for k in (rows, rows, len(heads) * s.head)]
    if not heads:
        shapes.pop()
    return list(
        pl.pallas_call(
            functools.partial(pack_kernel, s, index, heads),
            in_specs=[SMEM, HBM],
            out_specs=[ANY] * len(shapes),
            out_shape=shapes,
            scratch_shapes=[pltpu.VMEM(x.shape, BF16) for x in shapes]
            + [
                pltpu.VMEM((max(1, len(heads)), 2, s.rows, s.chip), BF16),
                pltpu.SemaphoreType.DMA((12,)),
            ],
            compiler_params=params(LIMITS[0]),
            cost_estimate=cost(0, 0),
            name="pack",
        )(idx, a)
    )


def gate_kernel(*refs):
    pass


def gate(buffers, tokens):
    n = len(buffers)
    return list(pl.pallas_call(
        gate_kernel,
        in_specs=[ANY] * (n + len(tokens)),
        out_specs=[ANY] * n,
        out_shape=[jax.ShapeDtypeStruct(b.shape, b.dtype) for b in buffers],
        input_output_aliases={i: i for i in range(n)},
        compiler_params=params(1),
        cost_estimate=cost(0, 0),
        name="gate",
    )(*buffers, *tokens))


def put_split(hi_ref, lo_ref, rows, cols, value):
    hi = value.astype(BF16)
    hi_ref[rows, cols] = hi
    if lo_ref is None:
        return
    rest = (value - hi.astype(F32)) * LOW
    lo_ref[rows, cols] = jnp.clip(rest, -F8_MAX, F8_MAX).astype(F8)


def prep_kernel(
    s, idx_ref, index_ref, grid_ref, mass_ref, alpha_ref, regions_ref, a_ref, _, hop_out, down_out, s0_hi, s0_lo, s1_ref
):
    chip, _ = own_part(idx_ref)
    r = s.rows
    level = grid_ref[index_ref[0]]
    for other in range(4):
        cols = columns(chip, other, s)
        regions = regions_ref[:, cols]
        mass = jnp.zeros(regions.shape, F32)
        for region in range(mass_ref.shape[0]):
            value = mass_ref[region] * (1.0 + alpha_ref[region] * level)
            mass = jnp.where(regions == region, value, mass)
        hop = 2.0 / (mass[:-1] + mass[1:])
        here = slice(other * s.chip, (other + 1) * s.chip)
        hop_out[:, here] = hop
        for index in (0, 1):
            down_out[index, here, :] = jnp.broadcast_to(hop[index : index + 1, :], (128, s.chip)).T
            for plane in (0, 1):
                part = a_ref[index, plane, :, cols].astype(F32) * hop[index : index + 1, :]
                rows = slice(plane * r, (plane + 1) * r)
                hi, lo = ((s0_hi, s0_lo), (s1_ref, None))[index]
                put_split(hi, lo, rows, here, part)


def full(x):
    return pl.BlockSpec(x.shape, lambda i: (0,) * x.ndim)


def prep(s, idx, a, regions, region_mass, region_alpha, energy_grid, energy_index, token):
    shapes = [
        jax.ShapeDtypeStruct((regions.shape[0] - 1, regions.shape[1]), F32),
        jax.ShapeDtypeStruct((regions.shape[0] - 1, regions.shape[1], 128), F32),
    ] + split_shapes(s) + split_shapes(s)[:1]
    return pl.pallas_call(
        functools.partial(prep_kernel, s),
        grid=(1,),
        in_specs=[SMEM] * 5
        + [full(regions), pl.BlockSpec((2,) + a.shape[1:], lambda i: (0, 0, 0, 0)), ANY],
        out_specs=[full(x) for x in shapes],
        out_shape=shapes,
        compiler_params=params(16),
        cost_estimate=cost(0, 0),
        name="prep",
    )(idx, energy_index, energy_grid, region_mass, region_alpha, regions, a, token)


def split_shapes(s):
    return [jax.ShapeDtypeStruct((s.chip, s.size), kind) for kind in (BF16, F8)]


PIECES = 40


def start_pieces(s, chip, core, index, rows_refs, sides, z_at, whole, diags, copies):
    r, m = s.rows, s.chip

    def cols(other):
        return pl.ds(other * m, m)

    for side, (offset, ref, (xs, ys, z)) in enumerate(
        zip((core * r, (1 - core) * r), rows_refs, sides)
    ):

        def rows(base):
            return pl.ds(pl.multiple_of(base + offset, 16), r)

        for other in range(4):
            copies.start(
                ref.at[index, :, :, columns(chip, other, s)], whole.at[:, rows(0), cols(other)]
            )
        for which, got, at in ((1, xs, 0), (2, ys, 0), (3, z, z_at)):
            copies.start(got.at[pl.ds(at, r), :], whole.at[0, rows(which * m), cols(which)])
            copies.start(got.at[pl.ds(at + r, DIAG), :], diags.at[which - 1, side])
            if which == 3:
                continue
            for plane in (0, 1):
                copies.start(
                    got.at[pl.ds(s.head + plane * r, r), :],
                    whole.at[plane, rows(which * m), cols(3)],
                )
            copies.start(
                got.at[pl.ds(s.head + 2 * r, r), :],
                whole.at[which - 1, rows(which * m), cols(3 - which)],
            )


def complete(s, whole, diags):
    m = s.chip
    row = lax.broadcasted_iota(jnp.int32, (m, m), 0)
    col = lax.broadcasted_iota(jnp.int32, (m, m), 1)
    for which in (1, 2, 3):
        here = slice(which * m, (which + 1) * m)
        packed = whole[0, here, here].astype(F32)
        flipped = packed.T
        diag = diags[which - 1, 0].astype(F32) + diags[which - 1, 1].astype(F32)
        diag = jnp.broadcast_to(diag[0:1, :], (m, m))
        real = jnp.where(col >= row, packed, flipped)
        imag = jnp.where(col < row, packed, jnp.where(col > row, flipped, diag))
        whole[0, here, here] = real.astype(BF16)
        whole[1, here, here] = imag.astype(BF16)
    for plane in (0, 1):
        for a, b in ((0, 1), (0, 2), (0, 3), (1, 3), (2, 3), (1, 2) if plane == 0 else (2, 1)):
            block = whole[plane, a * m : (a + 1) * m, b * m : (b + 1) * m]
            whole[plane, b * m : (b + 1) * m, a * m : (a + 1) * m] = block.T


def multiply(lefts, right, s):
    r = s.rows
    if any(lo is not None for _, lo in lefts):
        small = [jnp.clip(plane, -F8_MAX, F8_MAX).astype(F8) for plane in right]
    out = []
    for hi, lo in lefts:
        by = [jnp.dot(hi[...], plane, preferred_element_type=F32) for plane in right]
        if lo is not None:
            by = [
                part + jnp.dot(lo[...], low, preferred_element_type=F32) * (1.0 / LOW)
                for part, low in zip(by, small)
            ]
        out.append((by[0][:r] - by[1][r:], by[1][:r] + by[0][r:]))
    return out


def planes(whole, cols):
    return [whole[plane, :, cols] for plane in (0, 1)]


def segments(start, width, s):
    at, out = start, []
    while at < start + width:
        other = at // s.chip
        stop = min(start + width, (other + 1) * s.chip)
        out.append((at, stop - at, other, at - other * s.chip))
        at = stop
    return out


def first_kernel(s, idx_ref, hop_ref, down_ref, hi, lo, *refs):
    own, own_c, x1, x1_c, y1, y1_c, z, z_c = refs[:8]
    scaled, x, w_hi, w_lo, whole, diags, sems = refs[8:]
    chip, core = own_part(idx_ref)
    r, n = s.rows, s.size
    copies = Copies(sems)
    sides = ((x1, y1, z), (x1_c, y1_c, z_c))
    start_pieces(s, chip, core, 1, (own, own_c), sides, 0, whole, diags, copies)
    copies.wait()
    complete(s, whole, diags)
    for t in range(0, n, TILE):
        cols = slice(t, t + TILE)
        right = planes(whole, cols)
        (parts,) = multiply([(hi, lo)], right, s)
        for plane, part in enumerate(parts):
            here = slice(plane * r, (plane + 1) * r)
            x[here, cols] = part
            put_split(w_hi, w_lo, here, cols, part * hop_ref[1:2, cols])
            scaled[plane, :, cols] = scale_rows(right[plane], down_ref, 1)


def scale_rows(plane, down_ref, index):
    return (plane.astype(F32) * down_ref[index, :, 0:1]).astype(BF16)


def second_kernel(s, idx_ref, s1_ref, w_hi, w_lo, *refs):
    own, own_c, x2, x2_c, y2, y2_c, z, z_c = refs[:8]
    u_ref, y_hi, y_lo, whole, diags, sems = refs[8:]
    chip, core = own_part(idx_ref)
    r, n = s.rows, s.size
    copies = Copies(sems)
    sides = ((x2, y2, z), (x2_c, y2_c, z_c))
    start_pieces(s, chip, core, 2, (own, own_c), sides, s.head, whole, diags, copies)
    copies.wait()
    complete(s, whole, diags)
    for t in range(0, n, TILE):
        cols = slice(t, t + TILE)
        u, y = multiply([(s1_ref, None), (w_hi, w_lo)], planes(whole, cols), s)
        for plane in (0, 1):
            here = slice(plane * r, (plane + 1) * r)
            put_split(u_ref, None, here, cols, u[plane])
            put_split(y_hi, y_lo, here, cols, y[plane])


def third_kernel(s, hi, lo, scaled, x, v_hi, v_lo):
    r, n = s.rows, s.size
    for t in range(0, n, TILE):
        cols = slice(t, t + TILE)
        (parts,) = multiply([(hi, lo)], planes(scaled, cols), s)
        for plane in (0, 1):
            here = slice(plane * r, (plane + 1) * r)
            put_split(v_hi, v_lo, here, cols, x[here, cols] + parts[plane])


def start_own(s, chip, a_ref, index, own, copies):
    return [
        copies.start(
            a_ref.at[index, :, :, columns(chip, other, s)],
            own.at[:, :, pl.ds(other * s.chip, s.chip)],
        )
        for other in range(4)
    ]


def green_kernel(s, idx_ref, left, scaled, a_ref, g1, own, sems):
    chip, core = own_part(idx_ref)
    copies = Copies(sems)
    mine = start_own(s, chip, a_ref, 1, own, copies)
    copies.wait(mine)
    for t in range(0, s.size, WIDE):
        (parts,) = multiply([(left, None)], planes(scaled, slice(t, t + WIDE)), s)
        add_own(s, own, parts, t, WIDE, g1)


def add_own(s, own, parts, start, width, g_ref):
    cols = slice(start, start + width)
    for plane in (0, 1):
        g_ref[plane, :, cols] = own[plane, :, cols].astype(F32) + parts[plane]


def send_out(s, chip, start, width, g_ref, out_ref, index, copies):
    for at, size, other, offset in segments(start, width, s):
        base = jnp.bitwise_xor(chip, other) * s.chip + offset
        where = pl.ds(pl.multiple_of(base, 128), size)
        copies.start(g_ref.at[:, :, pl.ds(at, size)], out_ref.at[index, :, :, where])


def last_kernel(s, idx_ref, down_ref, hi, lo, g1, *refs):
    rows, rows_c, x0, x0_c, y0, y0_c, z, z_c = refs[:8]
    out_ref, whole, diags, own, g0, sems = refs[8:]
    chip, core = own_part(idx_ref)
    copies = Copies(sems)
    sides = ((x0, y0, z), (x0_c, y0_c, z_c))
    start_pieces(s, chip, core, 0, (rows, rows_c), sides, 0, whole, diags, copies)
    start_own(s, chip, rows, 0, own, copies)
    copies.wait()
    send_out(s, chip, 0, s.size, g1, out_ref, 1, copies)
    complete(s, whole, diags)
    width = TILE
    for t in range(0, s.size, width):
        cols = slice(t, t + width)
        right = [scale_rows(plane, down_ref, 0) for plane in planes(whole, cols)]
        (parts,) = multiply([(hi, lo)], right, s)
        add_own(s, own, parts, t, width, g0)
        send_out(s, chip, t, width, g0, out_ref, 0, copies)
    copies.wait()


def swap(x, mask, n=8):
    return lax.ppermute(x, "cols", [(i, i ^ mask) for i in range(n)])


def special(left_inverse, regions, region_mass, region_alpha, energy_grid, energy_index):
    a = left_inverse
    s = Sizes(a.shape[2], a.shape[3])
    idx = lax.axis_index("cols").astype(jnp.int32)[None]
    n, m, r = s.size, s.chip, s.rows

    a_cross = swap(a, 1)
    x1, y1, z = pack(s, idx, a, 1, (1, 2))
    x1, y1, z = swap(x1, 2), swap(y1, 4), swap(z, 6)
    x2, y2 = pack(s, idx, a, 2, ())
    x0, y0, z0 = pack(s, idx, a, 0, (0,))
    hop, down, s0_hi, s0_lo, s1 = prep(
        s, idx, a, regions, region_mass, region_alpha, energy_grid, energy_index, a_cross
    )
    x1, y1, z = gate([x1, y1, z], (hop, x0, x2))
    x2, y2 = swap(x2, 2), swap(y2, 4)
    z_cross = swap(z, 1)

    split = split_shapes(s)
    block = jax.ShapeDtypeStruct((2, n, n), BF16)
    whole = pltpu.VMEM(block.shape, BF16)
    diags = pltpu.VMEM((3, 2, DIAG, m), BF16)
    own = pltpu.VMEM((2, r, n), BF16)
    sems = pltpu.SemaphoreType.DMA((PIECES + 20,))

    def call(kernel, name, ins, pieces, out_specs, out_shape, scratch, limit):
        return pl.pallas_call(
            functools.partial(kernel, s),
            in_specs=[SMEM if x is idx else HBM if x is a else VMEM for x in ins]
            + [HBM if x is a or x is a_cross else ANY for x in pieces],
            out_specs=out_specs,
            out_shape=out_shape,
            scratch_shapes=scratch,
            compiler_params=params(limit),
            cost_estimate=cost(0, 0),
            name=name,
        )(*ins, *pieces)

    scaled, x, w_hi, w_lo = call(
        first_kernel,
        "first",
        [idx, hop, down, s0_hi, s0_lo],
        [a, a_cross, x1, swap(x1, 1), y1, swap(y1, 1), z, z_cross],
        [VMEM] * 4,
        [block, jax.ShapeDtypeStruct((m, n), F32)] + split,
        [whole, diags, sems],
        LIMITS[1],
    )
    x0, y0, z0 = gate([x0, y0, z0], (z_cross,))
    x0, y0, z0 = swap(x0, 2), swap(y0, 4), swap(z0, 6)
    x2, y2 = gate([x2, y2], (w_hi,))
    u, y_hi, y_lo = call(
        second_kernel,
        "second",
        [idx, s1, w_hi, w_lo],
        [a, a_cross, x2, swap(x2, 1), y2, swap(y2, 1), z, z_cross],
        [VMEM] * 3,
        split[:1] + split,
        [whole, diags, sems],
        LIMITS[2],
    )
    v_hi, v_lo = call(
        third_kernel, "third", [y_hi, y_lo, scaled, x], [], [VMEM] * 2, split, [], LIMITS[3]
    )
    x0, y0, z0 = gate([x0, y0, z0], (v_hi,))
    green = jax.ShapeDtypeStruct((2, r, n), F32)
    g1 = call(
        green_kernel, "green_1", [idx, u, scaled, a], [], VMEM, green, [own, sems], LIMITS[3]
    )
    return call(
        last_kernel,
        "green_0",
        [idx, down, v_hi, v_lo, g1],
        [a, a_cross, x0, swap(x0, 1), y0, swap(y0, 1), z0, swap(z0, 1)],
        HBM,
        jax.ShapeDtypeStruct((2, 2, r, n), F32),
        [whole, diags, own, pltpu.VMEM((2, r, n), F32), sems],
        LIMITS[4],
    )


def solution(mesh):
    def on_device(left_inverse, *rest):
        rows = left_inverse.shape[2]
        if mesh.shape["cols"] == 8 and left_inverse.shape[0] == 3 and rows % 64 == 0:
            return special(left_inverse, *rest)
        return general(left_inverse, *rest)

    in_specs = (P("energy", None, "cols", None), P(), P(), P(), P(), P("energy"))
    out_specs = P("energy", None, "cols", None)
    return jax.shard_map(
        on_device, mesh=mesh, in_specs=in_specs, out_specs=out_specs, check_vma=False
    )
```

```python
import functools

import jax
import jax.numpy as jnp
from jax import lax
from jax.experimental import pallas as pl
from jax.experimental.pallas import tpu as pltpu
from jax.sharding import PartitionSpec as P

F32 = jnp.float32
BF16 = jnp.bfloat16
F8 = jnp.float8_e5m2
F8_MAX = 57344.0
LOW = 512.0
DIAG = 16
ORDER = (1, 2, 0)
PAD = 16
VMEM = pl.BlockSpec(memory_space=pltpu.VMEM)
SMEM = pl.BlockSpec(memory_space=pltpu.SMEM)
ANY = pl.BlockSpec(memory_space=pl.ANY)
HBM = pl.BlockSpec(memory_space=pltpu.HBM)


def params(mib=56):
    return pltpu.CompilerParams(vmem_limit_bytes=mib * 2**20)


def cost(flops, moved):
    return pl.CostEstimate(flops=flops, bytes_accessed=moved, transcendentals=0)


def couplings(regions, region_mass, region_alpha, energy_grid, energy_index):
    level = jnp.sum(
        jnp.where(jnp.arange(energy_grid.shape[0]) == energy_index[0], energy_grid, 0.0)
    )
    onehot = (regions[:, :, None] == jnp.arange(region_mass.shape[0])[None, None, :]).astype(F32)
    per_region = region_mass * (1.0 + region_alpha * level)
    mass = jnp.sum(onehot * per_region[None, None, :], axis=2)
    return 2.0 / (mass[:-1] + mass[1:])


def product(left, right):
    real = jnp.dot(left[0], right[0], preferred_element_type=F32) - jnp.dot(
        left[1], right[1], preferred_element_type=F32
    )
    imag = jnp.dot(left[0], right[1], preferred_element_type=F32) + jnp.dot(
        left[1], right[0], preferred_element_type=F32
    )
    return jnp.stack([real, imag])


def general(left_inverse, regions, region_mass, region_alpha, energy_grid, energy_index):
    hop = couplings(regions, region_mass, region_alpha, energy_grid, energy_index)
    count, _, own_rows, _ = left_inverse.shape
    offset = lax.axis_index("cols") * own_rows
    own_hop = lax.dynamic_slice_in_dim(hop, offset, own_rows, 1)
    whole = [lax.all_gather(a, "cols", axis=1, tiled=True) for a in left_inverse[: count - 1]]
    next_green = left_inverse[count - 1]
    blocks = []
    for index in range(count - 2, -1, -1):
        panel = left_inverse[index]
        scaled = (hop[index][None, :, None] * whole[index].astype(F32)).astype(BF16)
        image = (own_hop[index][None, :, None] * product(next_green, scaled)).astype(BF16)
        image = lax.all_gather(image, "cols", axis=1, tiled=True)
        current = panel.astype(F32) + product(panel, image)
        blocks.append(current)
        next_green = current.astype(BF16)
    return jnp.stack(blocks[::-1])


TILE = 256
WIDE = 512
LIMITS = (16, 16, 22, 24, 20)


class Sizes:
    def __init__(self, rows, size):
        self.rows = rows
        self.chip = 2 * rows
        self.size = size
        self.head = rows + DIAG
        self.slab = rows * 4 + DIAG


def own_part(idx_ref):
    index = idx_ref[0]
    return lax.div(index, 2), lax.rem(index, 2)


def columns(chip, other, s):
    return pl.ds(pl.multiple_of(jnp.bitwise_xor(chip, other) * s.chip, 128), s.chip)


class Copies:
    def __init__(self, sems):
        self.sems = sems
        self.made = []

    def start(self, source, target):
        copy = pltpu.make_async_copy(source, target, self.sems.at[len(self.made)])
        copy.start()
        self.made.append([copy, False])
        return len(self.made) - 1

    def wait(self, which=None):
        for i in range(len(self.made)) if which is None else which:
            copy, done = self.made[i]
            if not done:
                copy.wait()
                self.made[i][1] = True


def pack_kernel(s, index, heads, idx_ref, a_ref, *refs):
    n = 3 if heads else 2
    outs, buffers, (planes, sems) = refs[:n], refs[n : 2 * n], refs[2 * n :]
    xs, ys = buffers[:2]
    chip, core = own_part(idx_ref)
    r = s.rows
    copies = Copies(sems)
    blocks = heads or (index,)
    loads = [
        copies.start(a_ref.at[block, :, :, columns(chip, 0, s)], planes.at[i])
        for i, block in enumerate(blocks)
    ]
    for plane in (0, 1):
        here = pl.ds(s.head + plane * r, r)
        copies.start(a_ref.at[index, plane, :, columns(chip, 2, s)], xs.at[here, :])
        copies.start(a_ref.at[index, plane, :, columns(chip, 1, s)], ys.at[here, :])
    here = pl.ds(s.head + 2 * r, r)
    copies.start(a_ref.at[index, 0, :, columns(chip, 3, s)], xs.at[here, :])
    copies.start(a_ref.at[index, 1, :, columns(chip, 3, s)], ys.at[here, :])
    row = lax.broadcasted_iota(jnp.int32, (r, s.chip), 0) + core * r
    col = lax.broadcasted_iota(jnp.int32, (r, s.chip), 1)
    for i, block in enumerate(blocks):
        copies.wait([loads[i]])
        real = planes[i, 0].astype(F32)
        imag = planes[i, 1].astype(F32)
        head = jnp.where(col >= row, real, imag).astype(BF16)
        diag = jnp.sum(jnp.where(col == row, imag, 0.0), axis=0, keepdims=True)
        diag = jnp.broadcast_to(diag, (DIAG, s.chip)).astype(BF16)
        places = [(xs, 0), (ys, 0)] if block == index else []
        if heads:
            places.append((buffers[2], i * s.head))
        for buffer, start in places:
            buffer[start : start + r, :] = head
            buffer[start + r : start + s.head, :] = diag
    for buffer in (xs, ys):
        if buffer.shape[0] > s.slab:
            buffer[s.slab :, :] = jnp.zeros((buffer.shape[0] - s.slab, s.chip), BF16)
    copies.wait()
    for buffer, out in zip(buffers, outs):
        copies.start(buffer, out)
    copies.wait()


def pack(s, idx, a, index, heads):
    rows = s.slab + PAD * ORDER.index(index)
    shapes = [jax.ShapeDtypeStruct((k, s.chip), BF16) for k in (rows, rows, len(heads) * s.head)]
    if not heads:
        shapes.pop()
    return list(
        pl.pallas_call(
            functools.partial(pack_kernel, s, index, heads),
            in_specs=[SMEM, HBM],
            out_specs=[ANY] * len(shapes),
            out_shape=shapes,
            scratch_shapes=[pltpu.VMEM(x.shape, BF16) for x in shapes]
            + [
                pltpu.VMEM((max(1, len(heads)), 2, s.rows, s.chip), BF16),
                pltpu.SemaphoreType.DMA((12,)),
            ],
            compiler_params=params(LIMITS[0]),
            cost_estimate=cost(0, 0),
            name="pack",
        )(idx, a)
    )


def gate_kernel(*refs):
    pass


def gate(buffers, tokens):
    n = len(buffers)
    return list(pl.pallas_call(
        gate_kernel,
        in_specs=[ANY] * (n + len(tokens)),
        out_specs=[ANY] * n,
        out_shape=[jax.ShapeDtypeStruct(b.shape, b.dtype) for b in buffers],
        input_output_aliases={i: i for i in range(n)},
        compiler_params=params(1),
        cost_estimate=cost(0, 0),
        name="gate",
    )(*buffers, *tokens))


def put_split(hi_ref, lo_ref, rows, cols, value):
    hi = value.astype(BF16)
    hi_ref[rows, cols] = hi
    if lo_ref is None:
        return
    rest = (value - hi.astype(F32)) * LOW
    lo_ref[rows, cols] = jnp.clip(rest, -F8_MAX, F8_MAX).astype(F8)


def prep_kernel(
    s, idx_ref, index_ref, grid_ref, mass_ref, alpha_ref, regions_ref, a_ref, _, hop_out, down_out, s0_hi, s0_lo, s1_ref
):
    chip, _ = own_part(idx_ref)
    r = s.rows
    level = grid_ref[index_ref[0]]
    for other in range(4):
        cols = columns(chip, other, s)
        regions = regions_ref[:, cols]
        mass = jnp.zeros(regions.shape, F32)
        for region in range(mass_ref.shape[0]):
            value = mass_ref[region] * (1.0 + alpha_ref[region] * level)
            mass = jnp.where(regions == region, value, mass)
        hop = 2.0 / (mass[:-1] + mass[1:])
        here = slice(other * s.chip, (other + 1) * s.chip)
        hop_out[:, here] = hop
        for index in (0, 1):
            down_out[index, here, :] = jnp.broadcast_to(hop[index : index + 1, :], (128, s.chip)).T
            for plane in (0, 1):
                part = a_ref[index, plane, :, cols].astype(F32) * hop[index : index + 1, :]
                rows = slice(plane * r, (plane + 1) * r)
                hi, lo = ((s0_hi, s0_lo), (s1_ref, None))[index]
                put_split(hi, lo, rows, here, part)


def full(x):
    return pl.BlockSpec(x.shape, lambda i: (0,) * x.ndim)


def prep(s, idx, a, regions, region_mass, region_alpha, energy_grid, energy_index, token):
    shapes = [
        jax.ShapeDtypeStruct((regions.shape[0] - 1, regions.shape[1]), F32),
        jax.ShapeDtypeStruct((regions.shape[0] - 1, regions.shape[1], 128), F32),
    ] + split_shapes(s) + split_shapes(s)[:1]
    return pl.pallas_call(
        functools.partial(prep_kernel, s),
        grid=(1,),
        in_specs=[SMEM] * 5
        + [full(regions), pl.BlockSpec((2,) + a.shape[1:], lambda i: (0, 0, 0, 0)), ANY],
        out_specs=[full(x) for x in shapes],
        out_shape=shapes,
        compiler_params=params(16),
        cost_estimate=cost(0, 0),
        name="prep",
    )(idx, energy_index, energy_grid, region_mass, region_alpha, regions, a, token)


def split_shapes(s):
    return [jax.ShapeDtypeStruct((s.chip, s.size), kind) for kind in (BF16, F8)]


PIECES = 40


def start_pieces(s, chip, core, index, rows_refs, sides, z_at, whole, diags, copies):
    r, m = s.rows, s.chip

    def cols(other):
        return pl.ds(other * m, m)

    for side, (offset, ref, (xs, ys, z)) in enumerate(
        zip((core * r, (1 - core) * r), rows_refs, sides)
    ):

        def rows(base):
            return pl.ds(pl.multiple_of(base + offset, 16), r)

        for other in range(4):
            copies.start(
                ref.at[index, :, :, columns(chip, other, s)], whole.at[:, rows(0), cols(other)]
            )
        for which, got, at in ((1, xs, 0), (2, ys, 0), (3, z, z_at)):
            copies.start(got.at[pl.ds(at, r), :], whole.at[0, rows(which * m), cols(which)])
            copies.start(got.at[pl.ds(at + r, DIAG), :], diags.at[which - 1, side])
            if which == 3:
                continue
            for plane in (0, 1):
                copies.start(
                    got.at[pl.ds(s.head + plane * r, r), :],
                    whole.at[plane, rows(which * m), cols(3)],
                )
            copies.start(
                got.at[pl.ds(s.head + 2 * r, r), :],
                whole.at[which - 1, rows(which * m), cols(3 - which)],
            )


def complete(s, whole, diags):
    m = s.chip
    row = lax.broadcasted_iota(jnp.int32, (m, m), 0)
    col = lax.broadcasted_iota(jnp.int32, (m, m), 1)
    for which in (1, 2, 3):
        here = slice(which * m, (which + 1) * m)
        packed = whole[0, here, here].astype(F32)
        flipped = packed.T
        diag = diags[which - 1, 0].astype(F32) + diags[which - 1, 1].astype(F32)
        diag = jnp.broadcast_to(diag[0:1, :], (m, m))
        real = jnp.where(col >= row, packed, flipped)
        imag = jnp.where(col < row, packed, jnp.where(col > row, flipped, diag))
        whole[0, here, here] = real.astype(BF16)
        whole[1, here, here] = imag.astype(BF16)
    for plane in (0, 1):
        for a, b in ((0, 1), (0, 2), (0, 3), (1, 3), (2, 3), (1, 2) if plane == 0 else (2, 1)):
            block = whole[plane, a * m : (a + 1) * m, b * m : (b + 1) * m]
            whole[plane, b * m : (b + 1) * m, a * m : (a + 1) * m] = block.T


def multiply(lefts, right, s):
    r = s.rows
    if any(lo is not None for _, lo in lefts):
        small = [jnp.clip(plane, -F8_MAX, F8_MAX).astype(F8) for plane in right]
    out = []
    for hi, lo in lefts:
        by = [jnp.dot(hi[...], plane, preferred_element_type=F32) for plane in right]
        if lo is not None:
            by = [
                part + jnp.dot(lo[...], low, preferred_element_type=F32) * (1.0 / LOW)
                for part, low in zip(by, small)
            ]
        out.append((by[0][:r] - by[1][r:], by[1][:r] + by[0][r:]))
    return out


def planes(whole, cols):
    return [whole[plane, :, cols] for plane in (0, 1)]


def segments(start, width, s):
    at, out = start, []
    while at < start + width:
        other = at // s.chip
        stop = min(start + width, (other + 1) * s.chip)
        out.append((at, stop - at, other, at - other * s.chip))
        at = stop
    return out


def first_kernel(s, idx_ref, hop_ref, down_ref, hi, lo, *refs):
    own, own_c, x1, x1_c, y1, y1_c, z, z_c = refs[:8]
    scaled, x, w_hi, w_lo, whole, diags, sems = refs[8:]
    chip, core = own_part(idx_ref)
    r, n = s.rows, s.size
    copies = Copies(sems)
    sides = ((x1, y1, z), (x1_c, y1_c, z_c))
    start_pieces(s, chip, core, 1, (own, own_c), sides, 0, whole, diags, copies)
    copies.wait()
    complete(s, whole, diags)
    for t in range(0, n, TILE):
        cols = slice(t, t + TILE)
        right = planes(whole, cols)
        (parts,) = multiply([(hi, lo)], right, s)
        for plane, part in enumerate(parts):
            here = slice(plane * r, (plane + 1) * r)
            x[here, cols] = part
            put_split(w_hi, w_lo, here, cols, part * hop_ref[1:2, cols])
            scaled[plane, :, cols] = scale_rows(right[plane], down_ref, 1)


def scale_rows(plane, down_ref, index):
    return (plane.astype(F32) * down_ref[index, :, 0:1]).astype(BF16)


def second_kernel(s, idx_ref, s1_ref, w_hi, w_lo, *refs):
    own, own_c, x2, x2_c, y2, y2_c, z, z_c = refs[:8]
    u_ref, y_hi, y_lo, whole, diags, sems = refs[8:]
    chip, core = own_part(idx_ref)
    r, n = s.rows, s.size
    copies = Copies(sems)
    sides = ((x2, y2, z), (x2_c, y2_c, z_c))
    start_pieces(s, chip, core, 2, (own, own_c), sides, s.head, whole, diags, copies)
    copies.wait()
    complete(s, whole, diags)
    for t in range(0, n, TILE):
        cols = slice(t, t + TILE)
        u, y = multiply([(s1_ref, None), (w_hi, w_lo)], planes(whole, cols), s)
        for plane in (0, 1):
            here = slice(plane * r, (plane + 1) * r)
            put_split(u_ref, None, here, cols, u[plane])
            put_split(y_hi, y_lo, here, cols, y[plane])


def third_kernel(s, hi, lo, scaled, x, v_hi, v_lo):
    r, n = s.rows, s.size
    for t in range(0, n, TILE):
        cols = slice(t, t + TILE)
        (parts,) = multiply([(hi, lo)], planes(scaled, cols), s)
        for plane in (0, 1):
            here = slice(plane * r, (plane + 1) * r)
            put_split(v_hi, v_lo, here, cols, x[here, cols] + parts[plane])


def start_own(s, chip, a_ref, index, own, copies):
    return [
        copies.start(
            a_ref.at[index, :, :, columns(chip, other, s)],
            own.at[:, :, pl.ds(other * s.chip, s.chip)],
        )
        for other in range(4)
    ]


def green_kernel(s, idx_ref, left, scaled, a_ref, g1, own, sems):
    chip, core = own_part(idx_ref)
    copies = Copies(sems)
    mine = start_own(s, chip, a_ref, 1, own, copies)
    copies.wait(mine)
    for t in range(0, s.size, WIDE):
        (parts,) = multiply([(left, None)], planes(scaled, slice(t, t + WIDE)), s)
        add_own(s, own, parts, t, WIDE, g1)


def add_own(s, own, parts, start, width, g_ref):
    cols = slice(start, start + width)
    for plane in (0, 1):
        g_ref[plane, :, cols] = own[plane, :, cols].astype(F32) + parts[plane]


def send_out(s, chip, start, width, g_ref, out_ref, index, copies):
    for at, size, other, offset in segments(start, width, s):
        base = jnp.bitwise_xor(chip, other) * s.chip + offset
        where = pl.ds(pl.multiple_of(base, 128), size)
        copies.start(g_ref.at[:, :, pl.ds(at, size)], out_ref.at[index, :, :, where])


def last_kernel(s, idx_ref, down_ref, hi, lo, g1, *refs):
    rows, rows_c, x0, x0_c, y0, y0_c, z, z_c = refs[:8]
    out_ref, whole, diags, own, g0, sems = refs[8:]
    chip, core = own_part(idx_ref)
    copies = Copies(sems)
    sides = ((x0, y0, z), (x0_c, y0_c, z_c))
    start_pieces(s, chip, core, 0, (rows, rows_c), sides, 0, whole, diags, copies)
    start_own(s, chip, rows, 0, own, copies)
    copies.wait()
    send_out(s, chip, 0, s.size, g1, out_ref, 1, copies)
    complete(s, whole, diags)
    width = TILE
    for t in range(0, s.size, width):
        cols = slice(t, t + width)
        right = [scale_rows(plane, down_ref, 0) for plane in planes(whole, cols)]
        (parts,) = multiply([(hi, lo)], right, s)
        add_own(s, own, parts, t, width, g0)
        send_out(s, chip, t, width, g0, out_ref, 0, copies)
    copies.wait()


def swap(x, mask, n=8):
    return lax.ppermute(x, "cols", [(i, i ^ mask) for i in range(n)])


def special(left_inverse, regions, region_mass, region_alpha, energy_grid, energy_index):
    a = left_inverse
    s = Sizes(a.shape[2], a.shape[3])
    idx = lax.axis_index("cols").astype(jnp.int32)[None]
    n, m, r = s.size, s.chip, s.rows

    a_cross = swap(a, 1)
    x1, y1, z = pack(s, idx, a, 1, (1, 2))
    x1, y1, z = swap(x1, 2), swap(y1, 4), swap(z, 6)
    x2, y2 = pack(s, idx, a, 2, ())
    x0, y0, z0 = pack(s, idx, a, 0, (0,))
    hop, down, s0_hi, s0_lo, s1 = prep(
        s, idx, a, regions, region_mass, region_alpha, energy_grid, energy_index, a_cross
    )
    x1, y1, z = gate([x1, y1, z], (hop, x0, x2))
    x2, y2 = swap(x2, 2), swap(y2, 4)
    z_cross = swap(z, 1)

    split = split_shapes(s)
    block = jax.ShapeDtypeStruct((2, n, n), BF16)
    whole = pltpu.VMEM(block.shape, BF16)
    diags = pltpu.VMEM((3, 2, DIAG, m), BF16)
    own = pltpu.VMEM((2, r, n), BF16)
    sems = pltpu.SemaphoreType.DMA((PIECES + 20,))

    def call(kernel, name, ins, pieces, out_specs, out_shape, scratch, limit):
        return pl.pallas_call(
            functools.partial(kernel, s),
            in_specs=[SMEM if x is idx else HBM if x is a else VMEM for x in ins]
            + [HBM if x is a or x is a_cross else ANY for x in pieces],
            out_specs=out_specs,
            out_shape=out_shape,
            scratch_shapes=scratch,
            compiler_params=params(limit),
            cost_estimate=cost(0, 0),
            name=name,
        )(*ins, *pieces)

    scaled, x, w_hi, w_lo = call(
        first_kernel,
        "first",
        [idx, hop, down, s0_hi, s0_lo],
        [a, a_cross, x1, swap(x1, 1), y1, swap(y1, 1), z, z_cross],
        [VMEM] * 4,
        [block, jax.ShapeDtypeStruct((m, n), F32)] + split,
        [whole, diags, sems],
        LIMITS[1],
    )
    x0, y0, z0 = gate([x0, y0, z0], (w_hi,))
    x0, y0, z0 = swap(x0, 2), swap(y0, 4), swap(z0, 6)
    x2, y2 = gate([x2, y2], (w_hi,))
    u, y_hi, y_lo = call(
        second_kernel,
        "second",
        [idx, s1, w_hi, w_lo],
        [a, a_cross, x2, swap(x2, 1), y2, swap(y2, 1), z, z_cross],
        [VMEM] * 3,
        split[:1] + split,
        [whole, diags, sems],
        LIMITS[2],
    )
    v_hi, v_lo = call(
        third_kernel, "third", [y_hi, y_lo, scaled, x], [], [VMEM] * 2, split, [], LIMITS[3]
    )
    x0, y0, z0 = gate([x0, y0, z0], (v_hi,))
    green = jax.ShapeDtypeStruct((2, r, n), F32)
    g1 = call(
        green_kernel, "green_1", [idx, u, scaled, a], [], VMEM, green, [own, sems], LIMITS[3]
    )
    return call(
        last_kernel,
        "green_0",
        [idx, down, v_hi, v_lo, g1],
        [a, a_cross, x0, swap(x0, 1), y0, swap(y0, 1), z0, swap(z0, 1)],
        HBM,
        jax.ShapeDtypeStruct((2, 2, r, n), F32),
        [whole, diags, own, pltpu.VMEM((2, r, n), F32), sems],
        LIMITS[4],
    )


def solution(mesh):
    def on_device(left_inverse, *rest):
        rows = left_inverse.shape[2]
        if mesh.shape["cols"] == 8 and left_inverse.shape[0] == 3 and rows % 64 == 0:
            return special(left_inverse, *rest)
        return general(left_inverse, *rest)

    in_specs = (P("energy", None, "cols", None), P(), P(), P(), P(), P("energy"))
    out_specs = P("energy", None, "cols", None)
    return jax.shard_map(
        on_device, mesh=mesh, in_specs=in_specs, out_specs=out_specs, check_vma=False
    )
```

```python
import functools

import jax
import jax.numpy as jnp
from jax import lax
from jax.experimental import pallas as pl
from jax.experimental.pallas import tpu as pltpu
from jax.sharding import PartitionSpec as P

F32 = jnp.float32
BF16 = jnp.bfloat16
F8 = jnp.float8_e5m2
F8_MAX = 57344.0
LOW = 512.0
DIAG = 16
ORDER = (1, 2, 0)
PAD = 16
VMEM = pl.BlockSpec(memory_space=pltpu.VMEM)
SMEM = pl.BlockSpec(memory_space=pltpu.SMEM)
ANY = pl.BlockSpec(memory_space=pl.ANY)
HBM = pl.BlockSpec(memory_space=pltpu.HBM)


def params(mib=56):
    return pltpu.CompilerParams(vmem_limit_bytes=mib * 2**20)


def cost(flops, moved):
    return pl.CostEstimate(flops=flops, bytes_accessed=moved, transcendentals=0)


def couplings(regions, region_mass, region_alpha, energy_grid, energy_index):
    level = jnp.sum(
        jnp.where(jnp.arange(energy_grid.shape[0]) == energy_index[0], energy_grid, 0.0)
    )
    onehot = (regions[:, :, None] == jnp.arange(region_mass.shape[0])[None, None, :]).astype(F32)
    per_region = region_mass * (1.0 + region_alpha * level)
    mass = jnp.sum(onehot * per_region[None, None, :], axis=2)
    return 2.0 / (mass[:-1] + mass[1:])


def product(left, right):
    real = jnp.dot(left[0], right[0], preferred_element_type=F32) - jnp.dot(
        left[1], right[1], preferred_element_type=F32
    )
    imag = jnp.dot(left[0], right[1], preferred_element_type=F32) + jnp.dot(
        left[1], right[0], preferred_element_type=F32
    )
    return jnp.stack([real, imag])


def general(left_inverse, regions, region_mass, region_alpha, energy_grid, energy_index):
    hop = couplings(regions, region_mass, region_alpha, energy_grid, energy_index)
    count, _, own_rows, _ = left_inverse.shape
    offset = lax.axis_index("cols") * own_rows
    own_hop = lax.dynamic_slice_in_dim(hop, offset, own_rows, 1)
    whole = [lax.all_gather(a, "cols", axis=1, tiled=True) for a in left_inverse[: count - 1]]
    next_green = left_inverse[count - 1]
    blocks = []
    for index in range(count - 2, -1, -1):
        panel = left_inverse[index]
        scaled = (hop[index][None, :, None] * whole[index].astype(F32)).astype(BF16)
        image = (own_hop[index][None, :, None] * product(next_green, scaled)).astype(BF16)
        image = lax.all_gather(image, "cols", axis=1, tiled=True)
        current = panel.astype(F32) + product(panel, image)
        blocks.append(current)
        next_green = current.astype(BF16)
    return jnp.stack(blocks[::-1])


TILE = 256
WIDE = 512
LIMITS = (16, 16, 22, 24, 20)


class Sizes:
    def __init__(self, rows, size):
        self.rows = rows
        self.chip = 2 * rows
        self.size = size
        self.head = rows + DIAG
        self.slab = rows * 4 + DIAG


def own_part(idx_ref):
    index = idx_ref[0]
    return lax.div(index, 2), lax.rem(index, 2)


def columns(chip, other, s):
    return pl.ds(pl.multiple_of(jnp.bitwise_xor(chip, other) * s.chip, 128), s.chip)


class Copies:
    def __init__(self, sems):
        self.sems = sems
        self.made = []

    def start(self, source, target):
        copy = pltpu.make_async_copy(source, target, self.sems.at[len(self.made)])
        copy.start()
        self.made.append([copy, False])
        return len(self.made) - 1

    def wait(self, which=None):
        for i in range(len(self.made)) if which is None else which:
            copy, done = self.made[i]
            if not done:
                copy.wait()
                self.made[i][1] = True


def pack_kernel(s, index, heads, idx_ref, a_ref, *refs):
    n = 3 if heads else 2
    outs, buffers, (planes, sems) = refs[:n], refs[n : 2 * n], refs[2 * n :]
    xs, ys = buffers[:2]
    chip, core = own_part(idx_ref)
    r = s.rows
    copies = Copies(sems)
    blocks = heads or (index,)
    loads = [
        copies.start(a_ref.at[block, :, :, columns(chip, 0, s)], planes.at[i])
        for i, block in enumerate(blocks)
    ]
    for plane in (0, 1):
        here = pl.ds(s.head + plane * r, r)
        copies.start(a_ref.at[index, plane, :, columns(chip, 2, s)], xs.at[here, :])
        copies.start(a_ref.at[index, plane, :, columns(chip, 1, s)], ys.at[here, :])
    here = pl.ds(s.head + 2 * r, r)
    copies.start(a_ref.at[index, 0, :, columns(chip, 3, s)], xs.at[here, :])
    copies.start(a_ref.at[index, 1, :, columns(chip, 3, s)], ys.at[here, :])
    row = lax.broadcasted_iota(jnp.int32, (r, s.chip), 0) + core * r
    col = lax.broadcasted_iota(jnp.int32, (r, s.chip), 1)
    for i, block in enumerate(blocks):
        copies.wait([loads[i]])
        real = planes[i, 0].astype(F32)
        imag = planes[i, 1].astype(F32)
        head = jnp.where(col >= row, real, imag).astype(BF16)
        diag = jnp.sum(jnp.where(col == row, imag, 0.0), axis=0, keepdims=True)
        diag = jnp.broadcast_to(diag, (DIAG, s.chip)).astype(BF16)
        places = [(xs, 0), (ys, 0)] if block == index else []
        if heads:
            places.append((buffers[2], i * s.head))
        for buffer, start in places:
            buffer[start : start + r, :] = head
            buffer[start + r : start + s.head, :] = diag
    for buffer in (xs, ys):
        if buffer.shape[0] > s.slab:
            buffer[s.slab :, :] = jnp.zeros((buffer.shape[0] - s.slab, s.chip), BF16)
    copies.wait()
    for buffer, out in zip(buffers, outs):
        copies.start(buffer, out)
    copies.wait()


def pack(s, idx, a, index, heads):
    rows = s.slab + PAD * ORDER.index(index)
    shapes = [jax.ShapeDtypeStruct((k, s.chip), BF16) for k in (rows, rows, len(heads) * s.head)]
    if not heads:
        shapes.pop()
    return list(
        pl.pallas_call(
            functools.partial(pack_kernel, s, index, heads),
            in_specs=[SMEM, HBM],
            out_specs=[ANY] * len(shapes),
            out_shape=shapes,
            scratch_shapes=[pltpu.VMEM(x.shape, BF16) for x in shapes]
            + [
                pltpu.VMEM((max(1, len(heads)), 2, s.rows, s.chip), BF16),
                pltpu.SemaphoreType.DMA((12,)),
            ],
            compiler_params=params(LIMITS[0]),
            cost_estimate=cost(0, 0),
            name="pack",
        )(idx, a)
    )


def gate_kernel(*refs):
    pass


def gate(buffers, tokens):
    n = len(buffers)
    return list(pl.pallas_call(
        gate_kernel,
        in_specs=[ANY] * (n + len(tokens)),
        out_specs=[ANY] * n,
        out_shape=[jax.ShapeDtypeStruct(b.shape, b.dtype) for b in buffers],
        input_output_aliases={i: i for i in range(n)},
        compiler_params=params(1),
        cost_estimate=cost(0, 0),
        name="gate",
    )(*buffers, *tokens))


def put_split(hi_ref, lo_ref, rows, cols, value):
    hi = value.astype(BF16)
    hi_ref[rows, cols] = hi
    if lo_ref is None:
        return
    rest = (value - hi.astype(F32)) * LOW
    lo_ref[rows, cols] = jnp.clip(rest, -F8_MAX, F8_MAX).astype(F8)


def prep_kernel(
    s, idx_ref, index_ref, grid_ref, mass_ref, alpha_ref, regions_ref, a_ref, _, hop_out, down_out, s0_hi, s0_lo, s1_ref
):
    chip, _ = own_part(idx_ref)
    r = s.rows
    level = grid_ref[index_ref[0]]
    for other in range(4):
        cols = columns(chip, other, s)
        regions = regions_ref[:, cols]
        mass = jnp.zeros(regions.shape, F32)
        for region in range(mass_ref.shape[0]):
            value = mass_ref[region] * (1.0 + alpha_ref[region] * level)
            mass = jnp.where(regions == region, value, mass)
        hop = 2.0 / (mass[:-1] + mass[1:])
        here = slice(other * s.chip, (other + 1) * s.chip)
        hop_out[:, here] = hop
        for index in (0, 1):
            down_out[index, here, :] = jnp.broadcast_to(hop[index : index + 1, :], (128, s.chip)).T
            for plane in (0, 1):
                part = a_ref[index, plane, :, cols].astype(F32) * hop[index : index + 1, :]
                rows = slice(plane * r, (plane + 1) * r)
                hi, lo = ((s0_hi, s0_lo), (s1_ref, None))[index]
                put_split(hi, lo, rows, here, part)


def full(x):
    return pl.BlockSpec(x.shape, lambda i: (0,) * x.ndim)


def prep(s, idx, a, regions, region_mass, region_alpha, energy_grid, energy_index, token):
    shapes = [
        jax.ShapeDtypeStruct((regions.shape[0] - 1, regions.shape[1]), F32),
        jax.ShapeDtypeStruct((regions.shape[0] - 1, regions.shape[1], 128), F32),
    ] + split_shapes(s) + split_shapes(s)[:1]
    return pl.pallas_call(
        functools.partial(prep_kernel, s),
        grid=(1,),
        in_specs=[SMEM] * 5
        + [full(regions), pl.BlockSpec((2,) + a.shape[1:], lambda i: (0, 0, 0, 0)), ANY],
        out_specs=[full(x) for x in shapes],
        out_shape=shapes,
        compiler_params=params(16),
        cost_estimate=cost(0, 0),
        name="prep",
    )(idx, energy_index, energy_grid, region_mass, region_alpha, regions, a, token)


def split_shapes(s):
    return [jax.ShapeDtypeStruct((s.chip, s.size), kind) for kind in (BF16, F8)]


PIECES = 40


def start_pieces(s, chip, core, index, rows_refs, sides, z_at, whole, diags, copies):
    r, m = s.rows, s.chip

    def cols(other):
        return pl.ds(other * m, m)

    for side, (offset, ref, (xs, ys, z)) in enumerate(
        zip((core * r, (1 - core) * r), rows_refs, sides)
    ):

        def rows(base):
            return pl.ds(pl.multiple_of(base + offset, 16), r)

        for other in range(4):
            copies.start(
                ref.at[index, :, :, columns(chip, other, s)], whole.at[:, rows(0), cols(other)]
            )
        for which, got, at in ((1, xs, 0), (2, ys, 0), (3, z, z_at)):
            copies.start(got.at[pl.ds(at, r), :], whole.at[0, rows(which * m), cols(which)])
            copies.start(got.at[pl.ds(at + r, DIAG), :], diags.at[which - 1, side])
            if which == 3:
                continue
            for plane in (0, 1):
                copies.start(
                    got.at[pl.ds(s.head + plane * r, r), :],
                    whole.at[plane, rows(which * m), cols(3)],
                )
            copies.start(
                got.at[pl.ds(s.head + 2 * r, r), :],
                whole.at[which - 1, rows(which * m), cols(3 - which)],
            )


def complete(s, whole, diags):
    m = s.chip
    row = lax.broadcasted_iota(jnp.int32, (m, m), 0)
    col = lax.broadcasted_iota(jnp.int32, (m, m), 1)
    for which in (1, 2, 3):
        here = slice(which * m, (which + 1) * m)
        packed = whole[0, here, here]
        flipped = packed.T.astype(F32)
        packed = packed.astype(F32)
        diag = diags[which - 1, 0].astype(F32) + diags[which - 1, 1].astype(F32)
        diag = jnp.broadcast_to(diag[0:1, :], (m, m))
        real = jnp.where(col >= row, packed, flipped)
        imag = jnp.where(col < row, packed, jnp.where(col > row, flipped, diag))
        whole[0, here, here] = real.astype(BF16)
        whole[1, here, here] = imag.astype(BF16)
    for plane in (0, 1):
        for a, b in ((0, 1), (0, 2), (0, 3), (1, 3), (2, 3), (1, 2) if plane == 0 else (2, 1)):
            block = whole[plane, a * m : (a + 1) * m, b * m : (b + 1) * m]
            whole[plane, b * m : (b + 1) * m, a * m : (a + 1) * m] = block.T


def multiply(lefts, right, s):
    r = s.rows
    if any(lo is not None for _, lo in lefts):
        small = [jnp.clip(plane, -F8_MAX, F8_MAX).astype(F8) for plane in right]
    out = []
    for hi, lo in lefts:
        by = [jnp.dot(hi[...], plane, preferred_element_type=F32) for plane in right]
        if lo is not None:
            by = [
                part + jnp.dot(lo[...], low, preferred_element_type=F32) * (1.0 / LOW)
                for part, low in zip(by, small)
            ]
        out.append((by[0][:r] - by[1][r:], by[1][:r] + by[0][r:]))
    return out


def planes(whole, cols):
    return [whole[plane, :, cols] for plane in (0, 1)]


def segments(start, width, s):
    at, out = start, []
    while at < start + width:
        other = at // s.chip
        stop = min(start + width, (other + 1) * s.chip)
        out.append((at, stop - at, other, at - other * s.chip))
        at = stop
    return out


def first_kernel(s, idx_ref, hop_ref, down_ref, hi, lo, *refs):
    own, own_c, x1, x1_c, y1, y1_c, z, z_c = refs[:8]
    scaled, x, w_hi, w_lo, whole, diags, sems = refs[8:]
    chip, core = own_part(idx_ref)
    r, n = s.rows, s.size
    copies = Copies(sems)
    sides = ((x1, y1, z), (x1_c, y1_c, z_c))
    start_pieces(s, chip, core, 1, (own, own_c), sides, 0, whole, diags, copies)
    copies.wait()
    complete(s, whole, diags)
    for t in range(0, n, TILE):
        cols = slice(t, t + TILE)
        right = planes(whole, cols)
        (parts,) = multiply([(hi, lo)], right, s)
        for plane, part in enumerate(parts):
            here = slice(plane * r, (plane + 1) * r)
            x[here, cols] = part
            put_split(w_hi, w_lo, here, cols, part * hop_ref[1:2, cols])
            scaled[plane, :, cols] = scale_rows(right[plane], down_ref, 1)


def scale_rows(plane, down_ref, index):
    down = down_ref[index]
    down = jnp.concatenate([down] * (plane.shape[1] // down.shape[1]), axis=1)
    return (plane.astype(F32) * down).astype(BF16)


def second_kernel(s, idx_ref, s1_ref, w_hi, w_lo, *refs):
    own, own_c, x2, x2_c, y2, y2_c, z, z_c = refs[:8]
    u_ref, y_hi, y_lo, whole, diags, sems = refs[8:]
    chip, core = own_part(idx_ref)
    r, n = s.rows, s.size
    copies = Copies(sems)
    sides = ((x2, y2, z), (x2_c, y2_c, z_c))
    start_pieces(s, chip, core, 2, (own, own_c), sides, s.head, whole, diags, copies)
    copies.wait()
    complete(s, whole, diags)
    for t in range(0, n, TILE):
        cols = slice(t, t + TILE)
        u, y = multiply([(s1_ref, None), (w_hi, w_lo)], planes(whole, cols), s)
        for plane in (0, 1):
            here = slice(plane * r, (plane + 1) * r)
            put_split(u_ref, None, here, cols, u[plane])
            put_split(y_hi, y_lo, here, cols, y[plane])


def third_kernel(s, hi, lo, scaled, x, v_hi, v_lo):
    r, n = s.rows, s.size
    for t in range(0, n, TILE):
        cols = slice(t, t + TILE)
        (parts,) = multiply([(hi, lo)], planes(scaled, cols), s)
        for plane in (0, 1):
            here = slice(plane * r, (plane + 1) * r)
            put_split(v_hi, v_lo, here, cols, x[here, cols] + parts[plane])


def start_own(s, chip, a_ref, index, own, copies):
    return [
        copies.start(
            a_ref.at[index, :, :, columns(chip, other, s)],
            own.at[:, :, pl.ds(other * s.chip, s.chip)],
        )
        for other in range(4)
    ]


def green_kernel(s, idx_ref, left, scaled, a_ref, g1, own, sems):
    chip, core = own_part(idx_ref)
    copies = Copies(sems)
    mine = start_own(s, chip, a_ref, 1, own, copies)
    copies.wait(mine)
    for t in range(0, s.size, WIDE):
        (parts,) = multiply([(left, None)], planes(scaled, slice(t, t + WIDE)), s)
        add_own(s, own, parts, t, WIDE, g1)


def add_own(s, own, parts, start, width, g_ref):
    cols = slice(start, start + width)
    for plane in (0, 1):
        g_ref[plane, :, cols] = own[plane, :, cols].astype(F32) + parts[plane]


def send_out(s, chip, start, width, g_ref, out_ref, index, copies):
    for at, size, other, offset in segments(start, width, s):
        base = jnp.bitwise_xor(chip, other) * s.chip + offset
        where = pl.ds(pl.multiple_of(base, 128), size)
        copies.start(g_ref.at[:, :, pl.ds(at, size)], out_ref.at[index, :, :, where])


def last_kernel(s, idx_ref, down_ref, hi, lo, g1, *refs):
    rows, rows_c, x0, x0_c, y0, y0_c, z, z_c = refs[:8]
    out_ref, whole, diags, own, g0, sems = refs[8:]
    chip, core = own_part(idx_ref)
    copies = Copies(sems)
    sides = ((x0, y0, z), (x0_c, y0_c, z_c))
    start_pieces(s, chip, core, 0, (rows, rows_c), sides, 0, whole, diags, copies)
    start_own(s, chip, rows, 0, own, copies)
    copies.wait()
    send_out(s, chip, 0, s.size, g1, out_ref, 1, copies)
    complete(s, whole, diags)
    width = TILE
    for t in range(0, s.size, width):
        cols = slice(t, t + width)
        right = [scale_rows(plane, down_ref, 0) for plane in planes(whole, cols)]
        (parts,) = multiply([(hi, lo)], right, s)
        add_own(s, own, parts, t, width, g0)
        send_out(s, chip, t, width, g0, out_ref, 0, copies)
    copies.wait()


def swap(x, mask, n=8):
    return lax.ppermute(x, "cols", [(i, i ^ mask) for i in range(n)])


def special(left_inverse, regions, region_mass, region_alpha, energy_grid, energy_index):
    a = left_inverse
    s = Sizes(a.shape[2], a.shape[3])
    idx = lax.axis_index("cols").astype(jnp.int32)[None]
    n, m, r = s.size, s.chip, s.rows

    a_cross = swap(a, 1)
    x1, y1, z = pack(s, idx, a, 1, (1, 2))
    x1, y1, z = swap(x1, 2), swap(y1, 4), swap(z, 6)
    x2, y2 = pack(s, idx, a, 2, ())
    x0, y0, z0 = pack(s, idx, a, 0, (0,))
    hop, down, s0_hi, s0_lo, s1 = prep(
        s, idx, a, regions, region_mass, region_alpha, energy_grid, energy_index, a_cross
    )
    x1, y1, z = gate([x1, y1, z], (hop, x0, x2))
    x2, y2 = swap(x2, 2), swap(y2, 4)
    z_cross = swap(z, 1)

    split = split_shapes(s)
    block = jax.ShapeDtypeStruct((2, n, n), BF16)
    whole = pltpu.VMEM(block.shape, BF16)
    diags = pltpu.VMEM((3, 2, DIAG, m), BF16)
    own = pltpu.VMEM((2, r, n), BF16)
    sems = pltpu.SemaphoreType.DMA((PIECES + 20,))

    def call(kernel, name, ins, pieces, out_specs, out_shape, scratch, limit):
        return pl.pallas_call(
            functools.partial(kernel, s),
            in_specs=[SMEM if x is idx else HBM if x is a else VMEM for x in ins]
            + [HBM if x is a or x is a_cross else ANY for x in pieces],
            out_specs=out_specs,
            out_shape=out_shape,
            scratch_shapes=scratch,
            compiler_params=params(limit),
            cost_estimate=cost(0, 0),
            name=name,
        )(*ins, *pieces)

    scaled, x, w_hi, w_lo = call(
        first_kernel,
        "first",
        [idx, hop, down, s0_hi, s0_lo],
        [a, a_cross, x1, swap(x1, 1), y1, swap(y1, 1), z, z_cross],
        [VMEM] * 4,
        [block, jax.ShapeDtypeStruct((m, n), F32)] + split,
        [whole, diags, sems],
        LIMITS[1],
    )
    x0, y0, z0 = gate([x0, y0, z0], (w_hi,))
    x0, y0, z0 = swap(x0, 2), swap(y0, 4), swap(z0, 6)
    x2, y2 = gate([x2, y2], (w_hi,))
    u, y_hi, y_lo = call(
        second_kernel,
        "second",
        [idx, s1, w_hi, w_lo],
        [a, a_cross, x2, swap(x2, 1), y2, swap(y2, 1), z, z_cross],
        [VMEM] * 3,
        split[:1] + split,
        [whole, diags, sems],
        LIMITS[2],
    )
    v_hi, v_lo = call(
        third_kernel, "third", [y_hi, y_lo, scaled, x], [], [VMEM] * 2, split, [], LIMITS[3]
    )
    x0, y0, z0 = gate([x0, y0, z0], (v_hi,))
    green = jax.ShapeDtypeStruct((2, r, n), F32)
    g1 = call(
        green_kernel, "green_1", [idx, u, scaled, a], [], VMEM, green, [own, sems], LIMITS[3]
    )
    return call(
        last_kernel,
        "green_0",
        [idx, down, v_hi, v_lo, g1],
        [a, a_cross, x0, swap(x0, 1), y0, swap(y0, 1), z0, swap(z0, 1)],
        HBM,
        jax.ShapeDtypeStruct((2, 2, r, n), F32),
        [whole, diags, own, pltpu.VMEM((2, r, n), F32), sems],
        LIMITS[4],
    )


def solution(mesh):
    def on_device(left_inverse, *rest):
        rows = left_inverse.shape[2]
        if mesh.shape["cols"] == 8 and left_inverse.shape[0] == 3 and rows % 64 == 0:
            return special(left_inverse, *rest)
        return general(left_inverse, *rest)

    in_specs = (P("energy", None, "cols", None), P(), P(), P(), P(), P("energy"))
    out_specs = P("energy", None, "cols", None)
    return jax.shard_map(
        on_device, mesh=mesh, in_specs=in_specs, out_specs=out_specs, check_vma=False
    )
```
